32 devices in a mesh: pipe: 4 (over y, core), expert: 4 (over z), tensor: 2 (over x).
Axes of the slice: x: 2, y: 2, z: 4, core: 2. Of those that a mesh axis runs over, the one named last changes fastest.
Arguments:
- tokens: bfloat16 [64, 6144], P('expert', ('pipe', 'tensor')), may hold values from -6 to 6
- expert_ids: int32 [64, 2], P('expert'), may hold values from 0 to 3, all different within a row; in each aligned block of 16 rows (0 to 15, 16 to 31, ...) at most 10 rows name the same one
- gates: float32 [64, 2], P('expert'), may hold values from 0.2 to 1
- w_gate: bfloat16 [4, 6144, 8192], P('expert', None, ('pipe', 'tensor')), may hold values from -0.078125 to 0.078125
- w_up: bfloat16 [4, 6144, 8192], P('expert', None, ('pipe', 'tensor')), may hold values from -0.078125 to 0.078125
- w_down: bfloat16 [4, 8192, 6144], P('expert', ('pipe', 'tensor')), may hold values from -0.0625 to 0.0625
- d_out: bfloat16 [64, 6144], P('expert', ('pipe', 'tensor')), may hold values from -6 to 6
Outputs:
- moe_out: bfloat16 [64, 6144], P('expert', ('pipe', 'tensor'))
- grad_tokens: bfloat16 [64, 6144], P('expert', ('pipe', 'tensor'))
- grad_gates: float32 [64, 2], P('expert')
The draws below stay inside these ranges and needn't reach their ends.
Inputs may be any that keep to these rules, and one draw needn't show every extreme that they name: `expert_ids`: each row names 2 different experts. Among the rows of one index of expert (aligned blocks of 16 rows) no expert is named more than 10 times, a bound that some block reaches.
All inputs are finite; a program needn't handle non-finite values.
Results may differ from the reference program's by a relative error of at most 0.017.
Values may be sent and summed in bfloat16 or wider, within the bound.
A program may use at most 128 MiB of HBM per device.

```python
import math
import jax
import jax.numpy as jnp
import numpy as np
from jax import lax

D = 6144
HID = 8192
TOP = 2
TOK_DEV = 16
EXPERTS = 4
GROUP = 1
CAP = 10
TOKENS = 64
N_PIPE = 4
N_EXPERT = 4
N_TENSOR = 2


def block_levels(own_key, extent, cuts, low, largest):
    def one(dim, blocks):
        heights = jax.random.uniform(jax.random.fold_in(jax.random.fold_in(own_key, 6), dim), (blocks,), jnp.float32, low / len(cuts), largest / len(cuts))
        return jnp.repeat(jnp.exp(heights), extent[dim] // blocks).reshape((-1,) + (1,) * (len(extent) - dim - 1))

    loudness = one(*cuts[0])
    for cut in cuts[1:]:
        loudness = loudness * one(*cut)
    return loudness


def deal_out(own_key, own, number, rows, amount, top, bound, lean):
    sequence = jax.random.permutation(own_key, amount)
    heavy_load, usual = shares(amount, rows * top, bound, lean, True), shares(amount, rows * top, bound, lean, False)
    places = jnp.arange(amount)

    def named(sizes, offset_by):
        used = int((sizes > 0).sum())
        fixed = max(1, used // 4)
        moved = fixed + (places - fixed + offset_by * (used - fixed)) % max(1, amount - fixed)
        return jnp.zeros((amount,), jnp.int32).at[sequence[jnp.where(places < fixed, places, moved)]].set(jnp.asarray(sizes, jnp.int32))

    sizes = jnp.where(number % 4 == 0, named(heavy_load, number // 4), named(usual, number - number // 4 - 1))
    mixed = jax.random.permutation(jax.random.fold_in(own, 3), amount)
    donor, taker = mixed[0:amount // 2 * 2:2], mixed[1:amount // 2 * 2:2]
    slack = jnp.minimum(sizes[donor] - 1, bound - sizes[taker]) // 2
    slack = jnp.where((donor == sequence[0]) | (taker == sequence[0]) | (sizes[taker] == 0), 0, jnp.maximum(slack, 0))
    moved = jax.random.randint(jax.random.fold_in(own, 4), (amount // 2,), 0, 1 << 20) % (slack + 1)
    sizes = sizes.at[donor].add(-moved).at[taker].add(moved)
    items = jnp.searchsorted(jnp.cumsum(sizes), jnp.arange(rows * top), side="right").astype(jnp.int32)
    listing = items.reshape(top, rows).T
    listing = listing[jax.random.permutation(jax.random.fold_in(own, 1), rows)]
    offset_by = jax.random.randint(jax.random.fold_in(own, 2), (rows, 1), 0, top)
    return jnp.take_along_axis(listing, (jnp.arange(top)[None, :] + offset_by) % top, axis=1)


def shares(count, total, limit, slope, full):
    weights = [(1 << 20) // math.isqrt(standing ** slope) + 1 for standing in range(1, count + 1)]
    largest = limit if full else min(limit, max(-(-total // count), total * weights[0] // sum(weights)))
    least = 1 if total - largest >= count - 1 else 0
    counts, spare = [largest] + [least] * (count - 1), total - largest - least * (count - 1)
    while spare > 0:
        movable = [i for i in range(1, count) if counts[i] < largest] or [i for i in range(1, count) if counts[i] < limit]
        mass, left = sum([weights[i] for i in movable]), spare
        for i in movable:
            extra = min(limit - counts[i], max(1, left * weights[i] // mass), spare)
            counts[i] = counts[i] + extra
            spare = spare - extra
    return np.array(counts)


def gaussian(stream_key, extent, deviation, limit, cuts=(), kind=jnp.bfloat16):
    level = block_levels(stream_key, extent, cuts, -0.22, 0.18) if cuts else 1.0
    entries = jax.random.normal(stream_key, extent, jnp.float32) * deviation * level
    return jnp.minimum(jnp.maximum(entries, -limit), limit).astype(kind)


def setup_inputs(seed: int = 0) -> dict:
    keys = jax.random.split(jax.random.key(seed), 8)
    tokens = gaussian(keys[0], (TOKENS, D), 1.0, 6.0, ((0, 4), (1, 8)))
    expert_ids_keys = jax.random.split(jax.random.fold_in(keys[1], 1), TOKENS // TOK_DEV)
    expert_ids_turns = jax.random.permutation(jax.random.fold_in(keys[1], 3), TOKENS // TOK_DEV)
    expert_ids = jax.vmap(lambda own, number: deal_out(jax.random.fold_in(keys[1], 2), own, number, TOK_DEV, EXPERTS, TOP, CAP, 2))(expert_ids_keys, expert_ids_turns).reshape((TOKENS, TOP))
    gates = jnp.clip(0.2 + 0.8 * jax.random.uniform(keys[2], (TOKENS, TOP), jnp.float32) ** block_levels(keys[2], (TOKENS, TOP), ((0, 4),), -0.2, 0.2), 0.2, 1.0)
    w_gate = gaussian(keys[3], (EXPERTS * GROUP, D, HID // GROUP), D ** -0.5, 0.078125, ((0, 4), (2, 8)))
    w_up = gaussian(keys[4], (EXPERTS * GROUP, D, HID // GROUP), D ** -0.5, 0.078125, ((0, 4), (2, 8)))
    w_down = gaussian(keys[5], (EXPERTS * GROUP, HID // GROUP, D), HID ** -0.5, 0.0625, ((0, 4), (1, 8)))
    d_out = gaussian(keys[6], (TOKENS, D), 1.0, 6.0, ((0, 4), (1, 8)))
    return {"tokens": tokens, "expert_ids": expert_ids, "gates": gates, "w_gate": w_gate, "w_up": w_up, "w_down": w_down, "d_out": d_out}


def reference(tokens, expert_ids, gates, w_gate, w_up, w_down, d_out):
    blocks = N_EXPERT
    per_block = TOK_DEV * TOP
    ways = GROUP * N_PIPE * N_TENSOR
    block_hid = HID // ways
    group_hid = HID // GROUP
    full_gate = w_gate.reshape(EXPERTS, GROUP, D, group_hid).transpose(0, 2, 1, 3).reshape(EXPERTS, D, HID)
    full_up = w_up.reshape(EXPERTS, GROUP, D, group_hid).transpose(0, 2, 1, 3).reshape(EXPERTS, D, HID)
    full_down = w_down.reshape(EXPERTS, HID, D)
    flat = expert_ids.reshape(blocks, per_block)
    onehot = (flat[:, :, None] == jnp.arange(EXPERTS, dtype=jnp.int32)[None, None, :]).astype(jnp.int32)
    position = (jnp.sum(jnp.cumsum(onehot, axis=1) * onehot, axis=2) - 1).astype(jnp.int32)
    assign_index = jnp.arange(TOKENS * TOP, dtype=jnp.int32).reshape(blocks, per_block)
    block_index = jnp.broadcast_to(jnp.arange(blocks, dtype=jnp.int32)[:, None], (blocks, per_block))
    table = jnp.full((EXPERTS, blocks, CAP), -1, jnp.int32)
    table = table.at[flat, block_index, position].set(assign_index)
    table = table.reshape(EXPERTS, blocks * CAP)
    flat_gates = gates.reshape(-1)

    def expert(inputs):
        e_table, wg, wu, wd = inputs
        live = e_table >= 0
        safe = jnp.where(live, e_table, 0).astype(jnp.int32)
        tok_index = (safe // TOP).astype(jnp.int32)
        rows_x = tokens[tok_index] * live[:, None].astype(tokens.dtype)
        weight = jnp.where(live, flat_gates[safe], jnp.zeros((), flat_gates.dtype))
        rows_dy = (d_out[tok_index].astype(jnp.float32) * weight[:, None].astype(jnp.float32)).astype(jnp.bfloat16)
        h_gate = jnp.dot(rows_x, wg, preferred_element_type=jnp.float32)
        h_up = jnp.dot(rows_x, wu, preferred_element_type=jnp.float32)
        sig = jax.nn.sigmoid(h_gate)
        hidden = (h_gate * sig * h_up).astype(jnp.bfloat16)
        count = rows_x.shape[0]
        parts = jnp.einsum("rbh,bhd->brd", hidden.reshape(count, ways, block_hid).astype(jnp.float32),
                           wd.reshape(ways, block_hid, D).astype(jnp.float32), precision=lax.Precision.HIGHEST)
        parts = lax.optimization_barrier(parts.astype(jnp.bfloat16)).astype(jnp.float32)
        out = jnp.sum(parts, axis=0).astype(jnp.bfloat16)
        d_hidden = jnp.dot(rows_dy, wd.T, preferred_element_type=jnp.float32)
        d_gate_h = (d_hidden * h_up * sig * (1.0 + h_gate * (1.0 - sig))).astype(jnp.bfloat16)
        d_up_h = (d_hidden * h_gate * sig).astype(jnp.bfloat16)
        parts_dx = jnp.einsum("rbh,bhd->brd", d_gate_h.reshape(count, ways, block_hid).astype(jnp.float32),
                              wg.T.reshape(ways, block_hid, D).astype(jnp.float32), precision=lax.Precision.HIGHEST)
        parts_dx = parts_dx + jnp.einsum("rbh,bhd->brd", d_up_h.reshape(count, ways, block_hid).astype(jnp.float32),
                                         wu.T.reshape(ways, block_hid, D).astype(jnp.float32), precision=lax.Precision.HIGHEST)
        parts_dx = lax.optimization_barrier(parts_dx.astype(jnp.bfloat16)).astype(jnp.float32)
        grad_rows = jnp.sum(parts_dx, axis=0).astype(jnp.bfloat16)
        return out, grad_rows

    out_all, dx_all = lax.map(expert, (table, full_gate, full_up, full_down))
    slot_index = (block_index * CAP + position).reshape(-1).astype(jnp.int32)
    ids_flat = expert_ids.reshape(-1).astype(jnp.int32)
    a_out = out_all[ids_flat, slot_index].astype(jnp.float32).reshape(TOKENS, TOP, D)
    a_dx = dx_all[ids_flat, slot_index].astype(jnp.float32).reshape(TOKENS, TOP, D)
    moe_out = jnp.sum(gates[:, :, None].astype(jnp.float32) * a_out, axis=1).astype(jnp.bfloat16)
    grad_tokens = jnp.sum(a_dx, axis=1).astype(jnp.bfloat16)
    grad_gates = jnp.sum(d_out.astype(jnp.float32)[:, None, :] * a_out, axis=2)
    return moe_out, grad_tokens, grad_gates
```

```python
import functools
import jax
import jax.numpy as jnp
from jax import lax
from jax.experimental import pallas as pl
from jax.experimental.pallas import tpu as pltpu
from jax.sharding import PartitionSpec as P

MESH = pl.DeviceIdType.MESH
FLIPS = ((0, 0, 0), (1, 0, 0), (0, 1, 0), (0, 0, 1), (1, 1, 0), (1, 0, 1), (0, 1, 1), (1, 1, 1))
OWN, C, X, Y, CX, CY, XY, CXY = range(8)
NT = (((1,), (1,)), ((), ()))
TN = (((0,), (0,)), ((), ()))
F32, BF16 = jnp.float32, jnp.bfloat16


def layer_kernel(
    cap, pipe_n, expert_n, tensor_n,
    tok_ref, ids_ref, gates_ref, wg_ref, wu_ref, wd_ref, dout_ref,
    moe_ref, gtok_ref, ggate_ref,
    wg, wu, wd, send_a, recv_a, blocks, hg, hu, dh, hid, dgh, duh,
    to_core, from_core, keep, diag_out, diag_in, part_x, part_y, from_x, from_y,
    q_out, q_in, qz_out, qz_in, send_e, recv_e,
    w_sem, as_sem, ar_sem, gs_sem, gr_sem, cs_sem, cr_sem, ds_sem, dr_sem, fs_sem, fr_sem,
    qs_sem, qr_sem, zs_sem, zr_sem, es_sem, er_sem,
):
    p = lax.axis_index("pipe")
    z = lax.axis_index("expert")
    t = lax.axis_index("tensor")
    toks, feat = tok_ref.shape
    rows = expert_n * cap
    span = 2 * toks
    hidn = wg.shape[2]

    def plane(r):
        fc, fx, fy = FLIPS[r]
        core, y = lax.rem(p, 2), lax.div(p, 2)
        core = 1 - core if fc else core
        y = 1 - y if fy else y
        return y * 2 + core, (1 - t if fx else t)

    def at_plane(r):
        pp, tt = plane(r)
        return {"pipe": pp, "expert": z, "tensor": tt}

    def at_z(step):
        return {"pipe": p, "expert": lax.rem(z + step, expert_n), "tensor": t}

    loads = []
    for r in range(8):
        pp, tt = plane(r)
        off = pl.multiple_of((pp * tensor_n + tt) * feat, feat)
        three = (
            pltpu.make_async_copy(wg_ref.at[0, pl.ds(off, feat), :], wg.at[r], w_sem.at[r, 0]),
            pltpu.make_async_copy(wu_ref.at[0, pl.ds(off, feat), :], wu.at[r], w_sem.at[r, 1]),
            pltpu.make_async_copy(wd_ref.at[0, :, pl.ds(off, feat)], wd.at[r], w_sem.at[r, 2]),
        )
        for copy in three:
            copy.start()
        loads.append(three)

    barrier = pltpu.get_barrier_semaphore()
    for r in range(1, 8):
        pl.semaphore_signal(barrier, inc=1, device_id=at_plane(r), device_id_type=MESH)
    for step in range(1, expert_n):
        pl.semaphore_signal(barrier, inc=1, device_id=at_z(step), device_id_type=MESH)

    def remote(src, dst, ssem, rsem, where):
        return pltpu.make_async_remote_copy(
            src_ref=src, dst_ref=dst, send_sem=ssem, recv_sem=rsem,
            device_id=where, device_id_type=MESH,
        )

    lanes = expert_n * span
    lane = lax.broadcasted_iota(jnp.int32, (toks, lanes), 1)
    id0, id1 = ids_ref[:, 0:1], ids_ref[:, 1:2]
    g0, g1 = gates_ref[:, 0:1], gates_ref[:, 1:2]
    names = jnp.where((lane == id0) | (lane == id1), 1.0, 0.0).astype(BF16)
    earlier = jnp.where(
        lax.broadcasted_iota(jnp.int32, (toks, toks), 0) > lax.broadcasted_iota(jnp.int32, (toks, toks), 1),
        1.0, 0.0,
    ).astype(BF16)
    before = jnp.dot(earlier, names, preferred_element_type=F32)
    pos0 = jnp.sum(jnp.where(lane == id0, before, 0.0), axis=1, keepdims=True).astype(jnp.int32)
    pos1 = jnp.sum(jnp.where(lane == id1, before, 0.0), axis=1, keepdims=True).astype(jnp.int32)
    a0 = id0 * span + pos0
    a1 = id1 * span + pos1

    def hot(mask):
        return jnp.where(mask, 1.0, 0.0)

    pick = jnp.concatenate(
        [hot((lane == a0) | (lane == a1)), hot(lane == a0 + toks), hot(lane == a1 + toks)], axis=0
    ).astype(BF16)
    d_out = dout_ref[...].astype(F32)
    source = jnp.concatenate([tok_ref[...].astype(F32), g0 * d_out, g1 * d_out], axis=0).astype(BF16)
    send_a[...] = lax.dot_general(pick, source, TN, preferred_element_type=F32).astype(BF16)
    hg[...] = jnp.zeros_like(hg)
    hu[...] = jnp.zeros_like(hu)
    dh[...] = jnp.zeros_like(dh)

    pl.semaphore_wait(barrier, 7 + expert_n - 1)

    mine = pl.ds(pl.multiple_of(z * span, span), span)
    sends = []
    dispatch = []
    for step in (2, 1, 3) if expert_n == 4 else range(1, expert_n):
        to = pl.ds(pl.multiple_of(lax.rem(z + step, expert_n) * span, span), span)
        copy = remote(send_a.at[to], recv_a.at[mine], as_sem.at[step - 1], ar_sem.at[step - 1], at_z(step))
        copy.start()
        sends.append(copy)
        dispatch.append(copy)
    recv_a[mine, :] = send_a[mine, :]

    tgt = lax.broadcasted_iota(jnp.int32, (2 * rows, lanes), 0)
    src = lax.broadcasted_iota(jnp.int32, (2 * rows, lanes), 1)
    slot = lax.rem(src, toks)
    home = lax.div(lax.rem(src, span), toks) * rows + lax.div(src, span) * cap + slot
    pack = hot((tgt == home) & (slot < cap)).astype(BF16)
    for copy in dispatch:
        copy.wait_recv()
    blocks[OWN] = jnp.dot(pack, recv_a[...], preferred_element_type=F32).astype(BF16)

    xr = (rows + 15) // 16 * 16
    top, low = pl.ds(0, xr), pl.ds(xr, 2 * rows - xr)

    def gather(src, dst, k, r):
        copy = remote(src, dst, gs_sem.at[k], gr_sem.at[k], at_plane(r))
        copy.start()
        sends.append(copy)
        return copy

    step_n = min(512, hidn)

    def forward(r):
        for copy in loads[r]:
            copy.wait()
        xs = blocks[r, 0:xr, :]
        ys = blocks[r, 2 * rows - xr : 2 * rows, :]

        def body(n, carry):
            cols = pl.ds(pl.multiple_of(n * step_n, step_n), step_n)
            hg[:, cols] += jnp.dot(xs, wg[r, :, cols], preferred_element_type=F32)
            hu[:, cols] += jnp.dot(xs, wu[r, :, cols], preferred_element_type=F32)
            dh[:, cols] += lax.dot_general(ys, wd[r, cols, :], NT, preferred_element_type=F32)
            return carry

        lax.fori_loop(0, hidn // step_n, body, 0)

    on_x = gather(blocks.at[OWN], blocks.at[X], 0, X)
    on_y = gather(blocks.at[OWN], blocks.at[Y], 1, Y)
    on_c = gather(blocks.at[OWN], blocks.at[C], 2, C)
    forward(OWN)
    on_c.wait_recv()
    forward(C)
    on_x.wait_recv()
    low_xy = gather(blocks.at[X, low], blocks.at[XY, low], 3, Y)
    on_cx = gather(blocks.at[X], blocks.at[CX], 4, C)
    on_y.wait_recv()
    top_xy = gather(blocks.at[Y, top], blocks.at[XY, top], 5, X)
    on_cy = gather(blocks.at[Y], blocks.at[CY], 6, C)
    forward(X)
    forward(Y)
    low_xy.wait_recv()
    top_xy.wait_recv()
    on_cxy = gather(blocks.at[XY], blocks.at[CXY], 7, C)
    on_cx.wait_recv()
    forward(CX)
    on_cy.wait_recv()
    forward(CY)
    forward(XY)
    on_cxy.wait_recv()
    forward(CXY)

    h_gate, h_up = hg[0:rows, :], hu[0:rows, :]
    d_hidden = dh[xr - rows : xr, :]
    sig = jax.nn.sigmoid(h_gate)
    hidden = h_gate * sig * h_up
    hid[...] = hidden.astype(BF16)
    dgh[...] = (d_hidden * h_up * sig * (1.0 + h_gate * (1.0 - sig))).astype(BF16)
    duh[...] = (d_hidden * h_gate * sig).astype(BF16)
    inner = jnp.sum(hidden * d_hidden, axis=1, keepdims=True)
    diagonal = lax.broadcasted_iota(jnp.int32, (rows, 128), 0) == lax.broadcasted_iota(jnp.int32, (rows, 128), 1)
    q_row = jnp.sum(jnp.where(diagonal, inner, 0.0), axis=0, keepdims=True)
    q_out[...] = jnp.broadcast_to(q_row, q_out.shape)
    me = p * tensor_n + t
    q_in[me] = q_out[...]
    q_copies = []

    def partial(r):
        out = jnp.dot(hid[...], wd[r], preferred_element_type=F32)
        dx = lax.dot_general(dgh[...], wg[r], NT, preferred_element_type=F32)
        dx = dx + lax.dot_general(duh[...], wu[r], NT, preferred_element_type=F32)
        return jnp.concatenate([out, dx], axis=0)

    def core_share(i, r):
        to_core[i] = partial(r).astype(BF16)
        copy = remote(to_core.at[i], from_core.at[i], cs_sem.at[i], cr_sem.at[i], at_plane(C))
        copy.start()
        sends.append(copy)
        return copy

    def chip_sum(i, copy):
        copy.wait_recv()
        return keep[...] + from_core[i].astype(F32)

    def ship(src, dst, ssem, rsem, r):
        copy = remote(src, dst, ssem, rsem, at_plane(r))
        copy.start()
        sends.append(copy)
        return copy

    s0 = core_share(0, CXY)
    for r in range(1, 8):
        copy = remote(q_out, q_in.at[me], qs_sem.at[r - 1], qr_sem.at[r - 1], at_plane(r))
        copy.start()
        sends.append(copy)
        q_copies.append(copy)
    keep[...] = partial(XY)
    s1 = core_share(1, CX)
    diag_out[...] = chip_sum(0, s0).astype(BF16)
    diag_x = ship(diag_out.at[top], diag_in.at[top], ds_sem.at[0], dr_sem.at[0], X)
    diag_y = ship(diag_out.at[low], diag_in.at[low], ds_sem.at[1], dr_sem.at[1], Y)
    keep[...] = partial(X)
    s2 = core_share(2, CY)
    part_x[...] = chip_sum(1, s1)
    keep[...] = partial(Y)
    diag_out_x = part_x[0:xr, :].astype(BF16)
    to_core[4, 0:xr, :] = diag_out_x
    x_top = ship(to_core.at[4, top], from_x.at[top], fs_sem.at[0], fr_sem.at[0], X)
    s3 = core_share(3, C)
    part_y[...] = chip_sum(2, s2)
    to_core[5, xr : 2 * rows, :] = part_y[xr : 2 * rows, :].astype(BF16)
    y_low = ship(to_core.at[5, low], from_y.at[low], fs_sem.at[1], fr_sem.at[1], Y)
    diag_x.wait_recv()
    to_core[5, 0:xr, :] = (part_y[0:xr, :] + diag_in[0:xr, :].astype(F32)).astype(BF16)
    y_top = ship(to_core.at[5, top], from_y.at[top], fs_sem.at[2], fr_sem.at[2], Y)
    diag_y.wait_recv()
    to_core[4, xr : 2 * rows, :] = (
        part_x[xr : 2 * rows, :] + diag_in[xr : 2 * rows, :].astype(F32)
    ).astype(BF16)
    x_low = ship(to_core.at[4, low], from_x.at[low], fs_sem.at[3], fr_sem.at[3], X)
    keep[...] = partial(OWN)
    keep[...] = chip_sum(3, s3)

    for copy in q_copies:
        copy.wait_recv()
    total_q = q_in[0]
    for j in range(1, 8):
        total_q = total_q + q_in[j]
    qz_out[...] = total_q
    qz_in[z] = total_q
    back = []
    for step in range(1, expert_n):
        copy = remote(qz_out, qz_in.at[z], zs_sem.at[step - 1], zr_sem.at[step - 1], at_z(step))
        copy.start()
        sends.append(copy)
        back.append(copy)

    for copy in (x_top, y_low, y_top, x_low):
        copy.wait_recv()
    final = (keep[...] + from_x[...].astype(F32) + from_y[...].astype(F32)).astype(BF16)
    send_e[...] = lax.dot_general(pack, final, TN, preferred_element_type=F32).astype(BF16)
    for step in (2, 1, 3) if expert_n == 4 else range(1, expert_n):
        to = pl.ds(pl.multiple_of(lax.rem(z + step, expert_n) * span, span), span)
        copy = remote(send_e.at[to], recv_e.at[mine], es_sem.at[step - 1], er_sem.at[step - 1], at_z(step))
        copy.start()
        sends.append(copy)
        back.append(copy)
    recv_e[mine, :] = send_e[mine, :]
    take = jnp.concatenate(
        [hot(lane == a0), hot(lane == a1), hot((lane == a0 + toks) | (lane == a1 + toks))], axis=0
    ).astype(BF16)
    for copy in back:
        copy.wait_recv()
    got = jnp.dot(take, recv_e[...], preferred_element_type=F32)
    moe_ref[...] = (g0 * got[0:toks] + g1 * got[toks : 2 * toks]).astype(moe_ref.dtype)
    gtok_ref[...] = got[2 * toks : 3 * toks].astype(gtok_ref.dtype)
    place = lax.broadcasted_iota(jnp.int32, (toks, 128), 1) - z * cap
    sum0 = jnp.zeros((toks, 1), F32)
    sum1 = jnp.zeros((toks, 1), F32)
    for e in range(expert_n):
        row = qz_in[e][0:1, :]
        sum0 += jnp.sum(jnp.where((id0 == e) & (place == pos0), row, 0.0), axis=1, keepdims=True)
        sum1 += jnp.sum(jnp.where((id1 == e) & (place == pos1), row, 0.0), axis=1, keepdims=True)
    two = lax.broadcasted_iota(jnp.int32, (toks, 2), 1)
    ggate_ref[...] = jnp.where(two == 0, sum0 / g0, sum1 / g1)
    for copy in sends:
        copy.wait_send()


def fused(cap, pipe_n, expert_n, tensor_n, tokens, expert_ids, gates, w_gate, w_up, w_down, d_out):
    toks, feat = tokens.shape
    hidn = w_gate.shape[2]
    rows = expert_n * cap
    xr = (rows + 15) // 16 * 16
    span = 2 * toks
    vm = lambda *shape: pltpu.VMEM(shape, BF16)
    vf = lambda *shape: pltpu.VMEM(shape, F32)
    dma = lambda *shape: pltpu.SemaphoreType.DMA(shape)
    inside, outside = pl.BlockSpec(memory_space=pltpu.VMEM), pl.BlockSpec(memory_space=pl.ANY)
    return pl.pallas_call(
        functools.partial(layer_kernel, cap, pipe_n, expert_n, tensor_n),
        out_shape=(
            jax.ShapeDtypeStruct(tokens.shape, BF16),
            jax.ShapeDtypeStruct(tokens.shape, BF16),
            jax.ShapeDtypeStruct(gates.shape, F32),
        ),
        in_specs=[inside, inside, inside, outside, outside, outside, inside],
        out_specs=(inside, inside, inside),
        scratch_shapes=[
            vm(8, feat, hidn), vm(8, feat, hidn), vm(8, hidn, feat),
            vm(expert_n * span, feat), vm(expert_n * span, feat), vm(8, 2 * rows, feat),
            vf(xr, hidn), vf(xr, hidn), vf(xr, hidn),
            vm(rows, hidn), vm(rows, hidn), vm(rows, hidn),
            vm(6, 2 * rows, feat), vm(4, 2 * rows, feat), vf(2 * rows, feat),
            vm(2 * rows, feat), vm(2 * rows, feat), vf(2 * rows, feat), vf(2 * rows, feat),
            vm(2 * rows, feat), vm(2 * rows, feat),
            vf(8, 128), vf(8, 8, 128), vf(8, 128), vf(expert_n, 8, 128),
            vm(expert_n * span, feat), vm(expert_n * span, feat),
            dma(8, 3), dma(expert_n - 1), dma(expert_n - 1), dma(8), dma(8), dma(4), dma(4),
            dma(2), dma(2), dma(4), dma(4), dma(7), dma(7), dma(expert_n - 1), dma(expert_n - 1),
            dma(expert_n - 1), dma(expert_n - 1),
        ],
        compiler_params=pltpu.CompilerParams(
            collective_id=0, has_side_effects=True, vmem_limit_bytes=56 * 1024 * 1024
        ),
        cost_estimate=pl.CostEstimate(
            flops=12 * rows * 8 * feat * hidn, bytes_accessed=48 * feat * hidn, transcendentals=rows * hidn
        ),
        name="moe_layer",
    )(tokens, expert_ids, gates, w_gate, w_up, w_down, d_out)


def per_device(tokens, expert_ids, gates, w_gate, w_up, w_down, d_out):
    tok_rows = tokens.shape[0]
    top = expert_ids.shape[1]
    devices_all = lax.axis_size("expert")
    experts = min(8, devices_all)
    group = devices_all // experts
    capacity = min(
        tok_rows,
        max(2, max(5 * tok_rows * top // (4 * experts), (tok_rows * top + experts - 1) // experts)),
    )
    slots = experts * capacity
    flat_ids = expert_ids.reshape(-1)
    onehot = (flat_ids[:, None] == jnp.arange(experts, dtype=jnp.int32)[None, :]).astype(jnp.int32)
    position = jnp.sum(jnp.cumsum(onehot, axis=0) * onehot, axis=1) - 1
    slot_of = flat_ids * capacity + position
    picks = (jnp.arange(slots, dtype=jnp.int32)[:, None] == slot_of[None, :]).astype(jnp.float32)
    pick_rows = picks.reshape(slots, tok_rows, top)
    select_tok = jnp.sum(pick_rows, axis=2).astype(jnp.bfloat16)
    select_gate = jnp.sum(pick_rows * gates[None, :, :], axis=2)
    whole_x, whole_dy = (
        lax.all_gather(tokens, ("pipe", "tensor"), axis=1, tiled=True),
        lax.all_gather(d_out, ("pipe", "tensor"), axis=1, tiled=True),
    )
    picked = jnp.dot(select_tok, whole_x, preferred_element_type=jnp.float32).astype(jnp.bfloat16)
    send_x = jnp.repeat(picked.reshape(experts, capacity, -1), group, axis=0)
    scaled = jnp.dot(select_gate, whole_dy.astype(jnp.float32), precision=lax.Precision.HIGHEST)
    send_dy = jnp.repeat(scaled.astype(jnp.bfloat16).reshape(experts, capacity, -1), group, axis=0)
    recv_x, recv_dy = (
        lax.all_to_all(send_x, "expert", split_axis=0, concat_axis=0, tiled=True),
        lax.all_to_all(send_dy, "expert", split_axis=0, concat_axis=0, tiled=True),
    )
    rows_x = recv_x.reshape(devices_all * capacity, -1)
    rows_dy = recv_dy.reshape(devices_all * capacity, -1)
    gate_proj = w_gate[0]
    up_proj = w_up[0]
    down_proj = w_down[0]
    contract_last = (((1,), (1,)), ((), ()))
    h_gate = jnp.dot(rows_x, gate_proj, preferred_element_type=jnp.float32)
    h_up = jnp.dot(rows_x, up_proj, preferred_element_type=jnp.float32)
    sig = jax.nn.sigmoid(h_gate)
    hidden = (h_gate * sig * h_up).astype(jnp.bfloat16)
    out_terms = jnp.dot(hidden, down_proj, preferred_element_type=jnp.float32)
    d_hidden = lax.dot_general(
        rows_dy, down_proj, contract_last, preferred_element_type=jnp.float32
    )
    d_gate_h = (d_hidden * h_up * sig * (1.0 + h_gate * (1.0 - sig))).astype(jnp.bfloat16)
    d_up_h = (d_hidden * h_gate * sig).astype(jnp.bfloat16)
    dx_terms = lax.dot_general(
        d_gate_h, gate_proj, contract_last, preferred_element_type=jnp.float32
    )
    dx_terms = dx_terms + lax.dot_general(
        d_up_h, up_proj, contract_last, preferred_element_type=jnp.float32
    )
    out_share, dx_share = (
        lax.psum_scatter(
            out_terms.astype(jnp.bfloat16), ("pipe", "tensor"), scatter_dimension=1, tiled=True
        ).astype(jnp.float32),
        lax.psum_scatter(
            dx_terms.astype(jnp.bfloat16), ("pipe", "tensor"), scatter_dimension=1, tiled=True
        ).astype(jnp.float32),
    )
    out_slot = out_share.reshape(devices_all, capacity, -1)
    dx_slot = dx_share.reshape(devices_all, capacity, -1)
    back_out, back_dx = (
        lax.all_to_all(
            out_slot.astype(jnp.bfloat16), "expert", split_axis=0, concat_axis=0, tiled=True
        ).astype(out_slot.dtype),
        lax.all_to_all(
            dx_slot.astype(jnp.bfloat16), "expert", split_axis=0, concat_axis=0, tiled=True
        ).astype(dx_slot.dtype),
    )
    out_rows = (
        jnp.sum(back_out.reshape(experts, group, capacity, -1), axis=1)
        .astype(jnp.bfloat16)
        .reshape(slots, -1)
    )
    dx_rows = (
        jnp.sum(back_dx.reshape(experts, group, capacity, -1), axis=1)
        .astype(jnp.bfloat16)
        .reshape(slots, -1)
    )
    assign = picks.T.astype(jnp.bfloat16)
    a_out = jnp.dot(assign, out_rows, preferred_element_type=jnp.float32)
    a_dx = jnp.dot(assign, dx_rows, preferred_element_type=jnp.float32)
    a_out = a_out.reshape(tok_rows, top, -1)
    a_dx = a_dx.reshape(tok_rows, top, -1)
    moe_out = jnp.sum(gates[:, :, None] * a_out, axis=1).astype(jnp.bfloat16)
    grad_tokens = jnp.sum(a_dx, axis=1).astype(jnp.bfloat16)
    partial_dots = jnp.sum(d_out.astype(jnp.float32)[:, None, :] * a_out, axis=2)
    grad_gates = lax.psum(partial_dots, ("pipe", "tensor"))
    return (moe_out, grad_tokens, grad_gates)


def solution(mesh):
    pipe_n, expert_n, tensor_n = mesh.shape["pipe"], mesh.shape["expert"], mesh.shape["tensor"]

    def layer(*args):
        toks, top = args[1].shape
        cap = min(toks, max(2, max(5 * toks * top // (4 * expert_n), (toks * top + expert_n - 1) // expert_n)))
        rows = expert_n * cap
        fits = pipe_n == 4 and tensor_n == 2 and top == 2 and expert_n == 4
        if fits and toks % 16 == 0 and rows % 8 == 0 and rows <= 128:
            return fused(cap, pipe_n, expert_n, tensor_n, *args)
        return per_device(*args)

    return jax.shard_map(
        layer,
        mesh=mesh,
        in_specs=(
            P("expert", ("pipe", "tensor")),
            P("expert", None),
            P("expert", None),
            P("expert", None, ("pipe", "tensor")),
            P("expert", None, ("pipe", "tensor")),
            P("expert", ("pipe", "tensor"), None),
            P("expert", ("pipe", "tensor")),
        ),
        out_specs=(
            P("expert", ("pipe", "tensor")),
            P("expert", ("pipe", "tensor")),
            P("expert", None),
        ),
        check_vma=False,
    )
```

```python
import functools
import jax
import jax.numpy as jnp
from jax import lax
from jax.experimental import pallas as pl
from jax.experimental.pallas import tpu as pltpu
from jax.sharding import PartitionSpec as P

MESH = pl.DeviceIdType.MESH
FLIPS = ((0, 0, 0), (1, 0, 0), (0, 1, 0), (0, 0, 1), (1, 1, 0), (1, 0, 1), (0, 1, 1), (1, 1, 1))
OWN, C, X, Y, CX, CY, XY, CXY = range(8)
NT = (((1,), (1,)), ((), ()))
TN = (((0,), (0,)), ((), ()))
F32, BF16 = jnp.float32, jnp.bfloat16


def layer_kernel(
    cap, pipe_n, expert_n, tensor_n,
    tok_ref, ids_ref, gates_ref, wg_ref, wu_ref, wd_ref, dout_ref,
    moe_ref, gtok_ref, ggate_ref,
    wg, wu, wd, send_a, recv_a, blocks, hg, hu, dh, hid, dgh, duh,
    to_core, from_core, keep, diag_out, diag_in, part_x, part_y, from_x, from_y,
    q_out, q_in, qz_out, qz_in, send_e, recv_e,
    w_sem, as_sem, ar_sem, gs_sem, gr_sem, cs_sem, cr_sem, ds_sem, dr_sem, fs_sem, fr_sem,
    qs_sem, qr_sem, zs_sem, zr_sem, es_sem, er_sem,
):
    p = lax.axis_index("pipe")
    z = lax.axis_index("expert")
    t = lax.axis_index("tensor")
    toks, feat = tok_ref.shape
    rows = expert_n * cap
    span = 2 * toks
    hidn = wg.shape[2]

    def plane(r):
        fc, fx, fy = FLIPS[r]
        core, y = lax.rem(p, 2), lax.div(p, 2)
        core = 1 - core if fc else core
        y = 1 - y if fy else y
        return y * 2 + core, (1 - t if fx else t)

    def at_plane(r):
        pp, tt = plane(r)
        return {"pipe": pp, "expert": z, "tensor": tt}

    def at_z(step):
        return {"pipe": p, "expert": lax.rem(z + step, expert_n), "tensor": t}

    loads = []
    for r in range(8):
        pp, tt = plane(r)
        off = pl.multiple_of((pp * tensor_n + tt) * feat, feat)
        three = (
            pltpu.make_async_copy(wg_ref.at[0, pl.ds(off, feat), :], wg.at[r], w_sem.at[r, 0]),
            pltpu.make_async_copy(wu_ref.at[0, pl.ds(off, feat), :], wu.at[r], w_sem.at[r, 1]),
            pltpu.make_async_copy(wd_ref.at[0, :, pl.ds(off, feat)], wd.at[r], w_sem.at[r, 2]),
        )
        loads.append(three)

    def load(first, last):
        for three in loads[first:last]:
            for copy in three:
                copy.start()

    load(0, 2)

    barrier = pltpu.get_barrier_semaphore()
    for r in range(1, 8):
        pl.semaphore_signal(barrier, inc=1, device_id=at_plane(r), device_id_type=MESH)
    for step in range(1, expert_n):
        pl.semaphore_signal(barrier, inc=1, device_id=at_z(step), device_id_type=MESH)

    def remote(src, dst, ssem, rsem, where):
        return pltpu.make_async_remote_copy(
            src_ref=src, dst_ref=dst, send_sem=ssem, recv_sem=rsem,
            device_id=where, device_id_type=MESH,
        )

    eye = lax.broadcasted_iota(jnp.int32, (toks, toks), 0) == lax.broadcasted_iota(jnp.int32, (toks, toks), 1)

    def column(row):
        return jnp.sum(jnp.where(eye, row, 0.0), axis=1, keepdims=True)

    piece = send_a.shape[1] - feat
    cuts = feat // piece
    rest = 2 * cap - toks
    lanes = expert_n * span
    lane = lax.broadcasted_iota(jnp.int32, (toks, lanes), 1)
    ids = ids_ref[...].astype(F32)
    id0, id1 = column(ids[0:1]).astype(jnp.int32), column(ids[1:2]).astype(jnp.int32)
    g0, g1 = column(gates_ref[0:1, :]), column(gates_ref[1:2, :])
    names = jnp.where((lane == id0) | (lane == id1), 1.0, 0.0).astype(BF16)
    earlier = jnp.where(
        lax.broadcasted_iota(jnp.int32, (toks, toks), 0) > lax.broadcasted_iota(jnp.int32, (toks, toks), 1),
        1.0, 0.0,
    ).astype(BF16)
    before = jnp.dot(earlier, names, preferred_element_type=F32)
    pos0 = jnp.sum(jnp.where(lane == id0, before, 0.0), axis=1, keepdims=True).astype(jnp.int32)
    pos1 = jnp.sum(jnp.where(lane == id1, before, 0.0), axis=1, keepdims=True).astype(jnp.int32)
    a0 = id0 * span + pos0
    a1 = id1 * span + pos1

    def hot(mask):
        return jnp.where(mask, 1.0, 0.0)

    pick = jnp.concatenate(
        [hot((lane == a0) | (lane == a1)), hot(lane == a0 + cap), hot(lane == a1 + cap)], axis=0
    ).astype(BF16)
    d_out = dout_ref[...].astype(F32)
    source = jnp.concatenate([tok_ref[...].astype(F32), g0 * d_out, g1 * d_out], axis=0).astype(BF16)
    slots = lax.dot_general(pick, source, TN, preferred_element_type=F32).astype(BF16)
    for e in range(expert_n):
        send_a[e * toks : (e + 1) * toks, 0:feat] = slots[e * span : e * span + toks]
    msg = lax.broadcasted_iota(jnp.int32, (expert_n * toks, lanes), 0)
    slot_lane = lax.broadcasted_iota(jnp.int32, (expert_n * toks, lanes), 1)
    beside = jnp.zeros((expert_n * toks, piece), F32)
    for c in range(cuts):
        j = lax.rem(msg, toks) - c * rest
        fold = hot((j >= 0) & (j < rest) & (slot_lane == lax.div(msg, toks) * span + toks + j)).astype(BF16)
        beside = beside + jnp.dot(fold, slots[:, c * piece : (c + 1) * piece], preferred_element_type=F32)
    send_a[:, feat:] = beside.astype(BF16)
    hg[...] = jnp.zeros_like(hg)
    hu[...] = jnp.zeros_like(hu)
    dh[...] = jnp.zeros_like(dh)

    pl.semaphore_wait(barrier, 7 + expert_n - 1)

    mine = pl.ds(pl.multiple_of(z * toks, toks), toks)
    sends = []
    dispatch = []
    for step in (2, 1, 3) if expert_n == 4 else range(1, expert_n):
        to = pl.ds(pl.multiple_of(lax.rem(z + step, expert_n) * toks, toks), toks)
        copy = remote(send_a.at[to], recv_a.at[mine], as_sem.at[step - 1], ar_sem.at[step - 1], at_z(step))
        copy.start()
        sends.append(copy)
        dispatch.append(copy)
    load(2, 5)
    recv_a[mine, :] = send_a[mine, :]

    tgt = lax.broadcasted_iota(jnp.int32, (2 * rows, expert_n * toks), 0)
    src = lax.broadcasted_iota(jnp.int32, (2 * rows, expert_n * toks), 1)
    e_src, n_src = lax.div(src, toks), lax.rem(src, toks)
    pack = hot(tgt == e_src * cap + n_src + jnp.where(n_src < cap, 0, rows - cap)).astype(BF16)
    unfold = []
    for c in range(cuts):
        j = n_src - c * rest
        unfold.append(
            hot((j >= 0) & (j < rest) & (tgt == rows - cap + e_src * cap + toks + j)).astype(BF16)
        )

    def unpack(main, folded, message):
        out = jnp.dot(main, message[:, 0:feat], preferred_element_type=F32)
        extra = [jnp.dot(m, message[:, feat:], preferred_element_type=F32) for m in folded]
        return out + (jnp.concatenate(extra, axis=1) if cuts > 1 else extra[0])

    for copy in dispatch:
        copy.wait_recv()
    blocks[OWN] = unpack(pack, unfold, recv_a[...]).astype(BF16)

    xr = (rows + 15) // 16 * 16
    top, low = pl.ds(0, xr), pl.ds(xr, 2 * rows - xr)

    def gather(src, dst, k, r):
        copy = remote(src, dst, gs_sem.at[k], gr_sem.at[k], at_plane(r))
        copy.start()
        sends.append(copy)
        return copy

    step_n = min(512, hidn)

    def forward(r):
        for copy in loads[r]:
            copy.wait()
        xs = blocks[r, 0:xr, :]
        ys = blocks[r, 2 * rows - xr : 2 * rows, :]

        def body(n, carry):
            cols = pl.ds(pl.multiple_of(n * step_n, step_n), step_n)
            hg[:, cols] += jnp.dot(xs, wg[r, :, cols], preferred_element_type=F32)
            hu[:, cols] += jnp.dot(xs, wu[r, :, cols], preferred_element_type=F32)
            dh[:, cols] += lax.dot_general(ys, wd[r, cols, :], NT, preferred_element_type=F32)
            return carry

        lax.fori_loop(0, hidn // step_n, body, 0)

    x_first = gather(blocks.at[OWN, low], blocks.at[X, low], 0, X)
    y_first = gather(blocks.at[OWN, top], blocks.at[Y, top], 1, Y)
    x_then = gather(blocks.at[OWN, top], blocks.at[X, top], 8, X)
    y_then = gather(blocks.at[OWN, low], blocks.at[Y, low], 9, Y)
    on_c = gather(blocks.at[OWN], blocks.at[C], 2, C)
    load(5, 8)
    forward(OWN)
    x_first.wait_recv()
    low_xy = gather(blocks.at[X, low], blocks.at[XY, low], 3, Y)
    y_first.wait_recv()
    top_xy = gather(blocks.at[Y, top], blocks.at[XY, top], 5, X)
    on_c.wait_recv()
    forward(C)
    x_then.wait_recv()
    on_cx = gather(blocks.at[X], blocks.at[CX], 4, C)
    y_then.wait_recv()
    on_cy = gather(blocks.at[Y], blocks.at[CY], 6, C)
    forward(X)
    forward(Y)
    low_xy.wait_recv()
    top_xy.wait_recv()
    on_cxy = gather(blocks.at[XY], blocks.at[CXY], 7, C)
    on_cx.wait_recv()
    forward(CX)
    on_cy.wait_recv()
    forward(CY)
    forward(XY)
    on_cxy.wait_recv()
    forward(CXY)

    h_gate, h_up = hg[0:rows, :], hu[0:rows, :]
    d_hidden = dh[xr - rows : xr, :]
    sig = jax.nn.sigmoid(h_gate)
    hidden = h_gate * sig * h_up
    hid[...] = hidden.astype(BF16)
    dgh[...] = (d_hidden * h_up * sig * (1.0 + h_gate * (1.0 - sig))).astype(BF16)
    duh[...] = (d_hidden * h_gate * sig).astype(BF16)
    inner = jnp.sum(hidden * d_hidden, axis=1, keepdims=True)
    diagonal = lax.broadcasted_iota(jnp.int32, (rows, 128), 0) == lax.broadcasted_iota(jnp.int32, (rows, 128), 1)
    q_row = jnp.sum(jnp.where(diagonal, inner, 0.0), axis=0, keepdims=True)
    q_out[...] = jnp.broadcast_to(q_row, q_out.shape)
    me = p * tensor_n + t
    q_in[me] = q_out[...]
    q_copies = []

    def partial(r):
        out = jnp.dot(hid[...], wd[r], preferred_element_type=F32)
        dx = lax.dot_general(dgh[...], wg[r], NT, preferred_element_type=F32)
        dx = dx + lax.dot_general(duh[...], wu[r], NT, preferred_element_type=F32)
        return jnp.concatenate([out, dx], axis=0)

    def core_share(i, r):
        to_core[i] = partial(r).astype(BF16)
        copy = remote(to_core.at[i], from_core.at[i], cs_sem.at[i], cr_sem.at[i], at_plane(C))
        copy.start()
        sends.append(copy)
        return copy

    def chip_sum(i, copy):
        copy.wait_recv()
        return keep[...] + from_core[i].astype(F32)

    def ship(src, dst, ssem, rsem, r):
        copy = remote(src, dst, ssem, rsem, at_plane(r))
        copy.start()
        sends.append(copy)
        return copy

    s0 = core_share(0, CXY)
    for r in range(1, 8):
        copy = remote(q_out, q_in.at[me], qs_sem.at[r - 1], qr_sem.at[r - 1], at_plane(r))
        copy.start()
        sends.append(copy)
        q_copies.append(copy)
    keep[...] = partial(XY)
    s1 = core_share(1, CX)
    diag_out[...] = chip_sum(0, s0).astype(BF16)
    diag_x = ship(diag_out.at[top], diag_in.at[top], ds_sem.at[0], dr_sem.at[0], X)
    diag_y = ship(diag_out.at[low], diag_in.at[low], ds_sem.at[1], dr_sem.at[1], Y)
    keep[...] = partial(X)
    s2 = core_share(2, CY)
    part_x[...] = chip_sum(1, s1)
    keep[...] = partial(Y)
    diag_out_x = part_x[0:xr, :].astype(BF16)
    to_core[4, 0:xr, :] = diag_out_x
    x_top = ship(to_core.at[4, top], from_x.at[top], fs_sem.at[0], fr_sem.at[0], X)
    s3 = core_share(3, C)
    part_y[...] = chip_sum(2, s2)
    to_core[5, xr : 2 * rows, :] = part_y[xr : 2 * rows, :].astype(BF16)
    y_low = ship(to_core.at[5, low], from_y.at[low], fs_sem.at[1], fr_sem.at[1], Y)
    diag_x.wait_recv()
    to_core[5, 0:xr, :] = (part_y[0:xr, :] + diag_in[0:xr, :].astype(F32)).astype(BF16)
    y_top = ship(to_core.at[5, top], from_y.at[top], fs_sem.at[2], fr_sem.at[2], Y)
    diag_y.wait_recv()
    to_core[4, xr : 2 * rows, :] = (
        part_x[xr : 2 * rows, :] + diag_in[xr : 2 * rows, :].astype(F32)
    ).astype(BF16)
    x_low = ship(to_core.at[4, low], from_x.at[low], fs_sem.at[3], fr_sem.at[3], X)
    keep[...] = partial(OWN)
    keep[...] = chip_sum(3, s3)

    for copy in q_copies:
        copy.wait_recv()
    total_q = q_in[0]
    for j in range(1, 8):
        total_q = total_q + q_in[j]
    qz_out[...] = total_q
    qz_in[z] = total_q
    back = []
    for step in range(1, expert_n):
        copy = remote(qz_out, qz_in.at[z], zs_sem.at[step - 1], zr_sem.at[step - 1], at_z(step))
        copy.start()
        sends.append(copy)
        back.append(copy)

    for copy in (x_top, y_low, y_top, x_low):
        copy.wait_recv()
    final = (keep[...] + from_x[...].astype(F32) + from_y[...].astype(F32)).astype(BF16)
    send_e[:, 0:feat] = lax.dot_general(pack, final, TN, preferred_element_type=F32).astype(BF16)
    beside = jnp.zeros((expert_n * toks, piece), F32)
    for c in range(cuts):
        part = final[:, c * piece : (c + 1) * piece]
        beside = beside + lax.dot_general(unfold[c], part, TN, preferred_element_type=F32)
    send_e[:, feat:] = beside.astype(BF16)
    for step in (2, 1, 3) if expert_n == 4 else range(1, expert_n):
        to = pl.ds(pl.multiple_of(lax.rem(z + step, expert_n) * toks, toks), toks)
        copy = remote(send_e.at[to], recv_e.at[mine], es_sem.at[step - 1], er_sem.at[step - 1], at_z(step))
        copy.start()
        sends.append(copy)
        back.append(copy)
    recv_e[mine, :] = send_e[mine, :]
    at = lax.broadcasted_iota(jnp.int32, (toks, expert_n * toks), 1)

    def taken(c):
        def one(e, n):
            if c is None:
                return (n < toks) & (at == e * toks + n)
            return (n >= toks) & (at == e * toks + n - toks + c * rest)

        return jnp.concatenate(
            [hot(one(id0, pos0)), hot(one(id1, pos1)), hot(one(id0, pos0 + cap) | one(id1, pos1 + cap))], axis=0
        ).astype(BF16)

    take, take_folded = taken(None), [taken(c) for c in range(cuts)]
    for copy in back:
        copy.wait_recv()
    got = unpack(take, take_folded, recv_e[...])
    moe_ref[...] = (g0 * got[0:toks] + g1 * got[toks : 2 * toks]).astype(moe_ref.dtype)
    gtok_ref[...] = got[2 * toks : 3 * toks].astype(gtok_ref.dtype)
    place = lax.broadcasted_iota(jnp.int32, (toks, 128), 1) - z * cap
    sum0 = jnp.zeros((toks, 1), F32)
    sum1 = jnp.zeros((toks, 1), F32)
    for e in range(expert_n):
        row = qz_in[e][0:1, :]
        sum0 += jnp.sum(jnp.where((id0 == e) & (place == pos0), row, 0.0), axis=1, keepdims=True)
        sum1 += jnp.sum(jnp.where((id1 == e) & (place == pos1), row, 0.0), axis=1, keepdims=True)
    ggate_ref[0:1, :] = jnp.sum(jnp.where(eye, sum0 / g0, 0.0), axis=0, keepdims=True)
    ggate_ref[1:2, :] = jnp.sum(jnp.where(eye, sum1 / g1, 0.0), axis=0, keepdims=True)
    for copy in sends:
        copy.wait_send()


def finish_kernel(a, b, c, out_a, out_b, out_c, sem):
    copies = [
        pltpu.make_async_copy(src, dst, sem.at[i])
        for i, (src, dst) in enumerate(((a, out_a), (b, out_b), (c, out_c)))
    ]
    for copy in copies:
        copy.start()
    for copy in copies:
        copy.wait()


def fold_lanes(cap, toks, feat):
    rest = 2 * cap - toks
    return -(-feat // (toks // rest * 128)) * 128 if 0 < rest <= toks else 0


def fused(cap, pipe_n, expert_n, tensor_n, tokens, expert_ids, gates, w_gate, w_up, w_down, d_out):
    toks, feat = tokens.shape
    hidn = w_gate.shape[2]
    rows = expert_n * cap
    xr = (rows + 15) // 16 * 16
    wide = feat + fold_lanes(cap, toks, feat)
    vm = lambda *shape: pltpu.VMEM(shape, BF16)
    vf = lambda *shape: pltpu.VMEM(shape, F32)
    dma = lambda *shape: pltpu.SemaphoreType.DMA(shape)
    inside, outside = pl.BlockSpec(memory_space=pltpu.VMEM), pl.BlockSpec(memory_space=pl.ANY)
    results = pl.pallas_call(
        functools.partial(layer_kernel, cap, pipe_n, expert_n, tensor_n),
        out_shape=(
            jax.ShapeDtypeStruct(tokens.shape, BF16),
            jax.ShapeDtypeStruct(tokens.shape, BF16),
            jax.ShapeDtypeStruct(gates.shape[::-1], F32),
        ),
        in_specs=[inside, inside, inside, outside, outside, outside, inside],
        out_specs=(inside, inside, inside),
        scratch_shapes=[
            vm(8, feat, hidn), vm(8, feat, hidn), vm(8, hidn, feat),
            vm(expert_n * toks, wide), vm(expert_n * toks, wide), vm(8, 2 * rows, feat),
            vf(xr, hidn), vf(xr, hidn), vf(xr, hidn),
            vm(rows, hidn), vm(rows, hidn), vm(rows, hidn),
            vm(6, 2 * rows, feat), vm(4, 2 * rows, feat), vf(2 * rows, feat),
            vm(2 * rows, feat), vm(2 * rows, feat), vf(2 * rows, feat), vf(2 * rows, feat),
            vm(2 * rows, feat), vm(2 * rows, feat),
            vf(8, 128), vf(8, 8, 128), vf(8, 128), vf(expert_n, 8, 128),
            vm(expert_n * toks, wide), vm(expert_n * toks, wide),
            dma(8, 3), dma(expert_n - 1), dma(expert_n - 1), dma(10), dma(10), dma(4), dma(4),
            dma(2), dma(2), dma(4), dma(4), dma(7), dma(7), dma(expert_n - 1), dma(expert_n - 1),
            dma(expert_n - 1), dma(expert_n - 1),
        ],
        compiler_params=pltpu.CompilerParams(
            collective_id=0, has_side_effects=True, vmem_limit_bytes=56 * 1024 * 1024
        ),
        cost_estimate=pl.CostEstimate(
            flops=12 * rows * 8 * feat * hidn, bytes_accessed=48 * feat * hidn, transcendentals=rows * hidn
        ),
        name="moe_layer",
    )(tokens, expert_ids.T, gates.T, w_gate, w_up, w_down, d_out)
    moe_out, grad_tokens, grad_gates = pl.pallas_call(
        finish_kernel,
        out_shape=tuple(jax.ShapeDtypeStruct(r.shape, r.dtype) for r in results),
        in_specs=[outside] * 3,
        out_specs=(outside,) * 3,
        scratch_shapes=[dma(3)],
        compiler_params=pltpu.CompilerParams(vmem_limit_bytes=60 * 1024 * 1024),
        name="hand_over",
    )(*results)
    return moe_out, grad_tokens, grad_gates.T


def per_device(tokens, expert_ids, gates, w_gate, w_up, w_down, d_out):
    tok_rows = tokens.shape[0]
    top = expert_ids.shape[1]
    devices_all = lax.axis_size("expert")
    experts = min(8, devices_all)
    group = devices_all // experts
    capacity = min(
        tok_rows,
        max(2, max(5 * tok_rows * top // (4 * experts), (tok_rows * top + experts - 1) // experts)),
    )
    slots = experts * capacity
    flat_ids = expert_ids.reshape(-1)
    onehot = (flat_ids[:, None] == jnp.arange(experts, dtype=jnp.int32)[None, :]).astype(jnp.int32)
    position = jnp.sum(jnp.cumsum(onehot, axis=0) * onehot, axis=1) - 1
    slot_of = flat_ids * capacity + position
    picks = (jnp.arange(slots, dtype=jnp.int32)[:, None] == slot_of[None, :]).astype(jnp.float32)
    pick_rows = picks.reshape(slots, tok_rows, top)
    select_tok = jnp.sum(pick_rows, axis=2).astype(jnp.bfloat16)
    select_gate = jnp.sum(pick_rows * gates[None, :, :], axis=2)
    whole_x, whole_dy = (
        lax.all_gather(tokens, ("pipe", "tensor"), axis=1, tiled=True),
        lax.all_gather(d_out, ("pipe", "tensor"), axis=1, tiled=True),
    )
    picked = jnp.dot(select_tok, whole_x, preferred_element_type=jnp.float32).astype(jnp.bfloat16)
    send_x = jnp.repeat(picked.reshape(experts, capacity, -1), group, axis=0)
    scaled = jnp.dot(select_gate, whole_dy.astype(jnp.float32), precision=lax.Precision.HIGHEST)
    send_dy = jnp.repeat(scaled.astype(jnp.bfloat16).reshape(experts, capacity, -1), group, axis=0)
    recv_x, recv_dy = (
        lax.all_to_all(send_x, "expert", split_axis=0, concat_axis=0, tiled=True),
        lax.all_to_all(send_dy, "expert", split_axis=0, concat_axis=0, tiled=True),
    )
    rows_x = recv_x.reshape(devices_all * capacity, -1)
    rows_dy = recv_dy.reshape(devices_all * capacity, -1)
    gate_proj = w_gate[0]
    up_proj = w_up[0]
    down_proj = w_down[0]
    contract_last = (((1,), (1,)), ((), ()))
    h_gate = jnp.dot(rows_x, gate_proj, preferred_element_type=jnp.float32)
    h_up = jnp.dot(rows_x, up_proj, preferred_element_type=jnp.float32)
    sig = jax.nn.sigmoid(h_gate)
    hidden = (h_gate * sig * h_up).astype(jnp.bfloat16)
    out_terms = jnp.dot(hidden, down_proj, preferred_element_type=jnp.float32)
    d_hidden = lax.dot_general(
        rows_dy, down_proj, contract_last, preferred_element_type=jnp.float32
    )
    d_gate_h = (d_hidden * h_up * sig * (1.0 + h_gate * (1.0 - sig))).astype(jnp.bfloat16)
    d_up_h = (d_hidden * h_gate * sig).astype(jnp.bfloat16)
    dx_terms = lax.dot_general(
        d_gate_h, gate_proj, contract_last, preferred_element_type=jnp.float32
    )
    dx_terms = dx_terms + lax.dot_general(
        d_up_h, up_proj, contract_last, preferred_element_type=jnp.float32
    )
    out_share, dx_share = (
        lax.psum_scatter(
            out_terms.astype(jnp.bfloat16), ("pipe", "tensor"), scatter_dimension=1, tiled=True
        ).astype(jnp.float32),
        lax.psum_scatter(
            dx_terms.astype(jnp.bfloat16), ("pipe", "tensor"), scatter_dimension=1, tiled=True
        ).astype(jnp.float32),
    )
    out_slot = out_share.reshape(devices_all, capacity, -1)
    dx_slot = dx_share.reshape(devices_all, capacity, -1)
    back_out, back_dx = (
        lax.all_to_all(
            out_slot.astype(jnp.bfloat16), "expert", split_axis=0, concat_axis=0, tiled=True
        ).astype(out_slot.dtype),
        lax.all_to_all(
            dx_slot.astype(jnp.bfloat16), "expert", split_axis=0, concat_axis=0, tiled=True
        ).astype(dx_slot.dtype),
    )
    out_rows = (
        jnp.sum(back_out.reshape(experts, group, capacity, -1), axis=1)
        .astype(jnp.bfloat16)
        .reshape(slots, -1)
    )
    dx_rows = (
        jnp.sum(back_dx.reshape(experts, group, capacity, -1), axis=1)
        .astype(jnp.bfloat16)
        .reshape(slots, -1)
    )
    assign = picks.T.astype(jnp.bfloat16)
    a_out = jnp.dot(assign, out_rows, preferred_element_type=jnp.float32)
    a_dx = jnp.dot(assign, dx_rows, preferred_element_type=jnp.float32)
    a_out = a_out.reshape(tok_rows, top, -1)
    a_dx = a_dx.reshape(tok_rows, top, -1)
    moe_out = jnp.sum(gates[:, :, None] * a_out, axis=1).astype(jnp.bfloat16)
    grad_tokens = jnp.sum(a_dx, axis=1).astype(jnp.bfloat16)
    partial_dots = jnp.sum(d_out.astype(jnp.float32)[:, None, :] * a_out, axis=2)
    grad_gates = lax.psum(partial_dots, ("pipe", "tensor"))
    return (moe_out, grad_tokens, grad_gates)


def solution(mesh):
    pipe_n, expert_n, tensor_n = mesh.shape["pipe"], mesh.shape["expert"], mesh.shape["tensor"]

    def layer(*args):
        toks, top = args[1].shape
        cap = min(toks, max(2, max(5 * toks * top // (4 * expert_n), (toks * top + expert_n - 1) // expert_n)))
        rows = expert_n * cap
        fits = pipe_n == 4 and tensor_n == 2 and top == 2 and expert_n == 4
        feat = args[0].shape[1]
        piece = fold_lanes(cap, toks, feat)
        fits = fits and cap < toks and piece > 0 and feat % piece == 0
        if fits and toks % 16 == 0 and rows % 8 == 0 and rows <= 128:
            return fused(cap, pipe_n, expert_n, tensor_n, *args)
        return per_device(*args)

    return jax.shard_map(
        layer,
        mesh=mesh,
        in_specs=(
            P("expert", ("pipe", "tensor")),
            P("expert", None),
            P("expert", None),
            P("expert", None, ("pipe", "tensor")),
            P("expert", None, ("pipe", "tensor")),
            P("expert", ("pipe", "tensor"), None),
            P("expert", ("pipe", "tensor")),
        ),
        out_specs=(
            P("expert", ("pipe", "tensor")),
            P("expert", ("pipe", "tensor")),
            P("expert", None),
        ),
        check_vma=False,
    )
```
